512 devices in a mesh: prow: 16 (over z), pcol: 32 (over y, x, core).
Axes of the slice: x: 4, y: 4, z: 16, core: 2. Of those that a mesh axis runs over, the one named last changes fastest.
Arguments:
- diag_inverse: float32 [8, 2048, 2048], P(None, 'pcol', 'prow'), as said below
- off_blocks: bfloat16 [28, 2048, 2048], P(None, 'pcol', 'prow'), may hold values from -0.046875 to 0.046875
- low_factor: bfloat16 [49152, 8, 2048], P('pcol', None, 'prow'), may hold values from -0.09375 to 0.09375
- rhs_top: float32 [8, 2048, 256], P(None, 'pcol'), may hold values from -6 to 6
- rhs_low: float32 [49152, 256], P(('pcol', 'prow')), may hold values from -6 to 6
Outputs:
- solved: float32 [8, 2048, 256], P(None, ('prow', 'pcol'))
- remaining: float32 [49152, 256], P(('pcol', 'prow'))
The draws below stay inside these ranges and needn't reach their ends.
Inputs may be any that keep to these rules, and one draw needn't show every extreme that they name: diag_inverse[k, c, r] is entry (r, c) of the inverse of the k-th diagonal factor block: lower triangular in (r, c), zero where c > r, diagonal between 1 and 2.
All inputs are finite; a program needn't handle non-finite values.
Results may differ from the reference program's by a relative error of at most 0.0059.
Values sent between devices are 32-bit elements; how exact they have to be, the bound alone decides.
A program may use at most 64 MiB of HBM per device.

```python
import math
import jax
import jax.numpy as jnp
from jax import lax

NB = 2048
PANELS = 8
R = 256
LOW_DEV = 1536
TRAIL = 49152
PAIRS = 28


def draw_diag_inverse(key, part):
    key = jax.random.fold_in(key, 11)
    diag_key, lower_key = jax.random.split(key)
    shape = (PANELS, NB, NB)
    column_idx = lax.broadcasted_iota(jnp.int32, shape, 1)
    row_idx = lax.broadcasted_iota(jnp.int32, shape, 2)
    diagonal = jax.random.uniform(diag_key, shape, jnp.float32, 1.0, 2.0)
    lower = jax.random.normal(lower_key, shape, jnp.float32)
    lower = lower * (0.5 / math.sqrt(NB))
    return jnp.where(column_idx == row_idx, diagonal, jnp.where(column_idx < row_idx, lower, 0.0)).astype(jnp.float32)


def raised(values, own_key, source, target, shards_of, factor):
    def block_of(dim):
        return (jnp.arange(values.shape[dim]) // (values.shape[dim] // shards_of)).reshape((-1,) + (1,) * (values.ndim - 1 - dim))

    near = jax.random.permutation(own_key, shards_of)[block_of(target)]
    other_side = (block_of(target) + shards_of // 2) % shards_of
    return jnp.where((block_of(source) == near) | (block_of(source) == other_side), factor * values, values)


def steps_of(stream_key, shape, shards, smallest, largest):
    def one(position, blocks):
        steps = jax.random.uniform(jax.random.fold_in(jax.random.fold_in(stream_key, 6), position), (blocks,), jnp.float32, smallest / len(shards), largest / len(shards))
        return jnp.repeat(jnp.exp(steps), shape[position] // blocks).reshape((-1,) + (1,) * (len(shape) - position - 1))

    loudness = one(*shards[0])
    for cut in shards[1:]:
        loudness = loudness * one(*cut)
    return loudness


def centred(rng, dims, deviation, reach, cuts=(), kind=jnp.bfloat16):
    gain = steps_of(rng, dims, cuts, -0.22, 0.18) if cuts else 1.0
    entries = jax.random.normal(rng, dims, jnp.float32) * deviation * gain
    return jnp.minimum(jnp.maximum(entries, -reach), reach).astype(kind)


def noise_with(key, shape, scale, reach, cuts, heavy, kind=jnp.bfloat16):
    result = scale * jax.random.normal(key, shape, jnp.float32)
    if cuts:
        result = result * steps_of(key, shape, cuts, -0.22, 0.18)
    return jnp.clip(raised(result, jax.random.fold_in(key, 3), *heavy), -reach, reach).astype(kind)


def setup_inputs(seed: int = 0) -> dict:
    splits = jax.random.split(jax.random.key(seed), 6)
    return {
        "diag_inverse": draw_diag_inverse(jax.random.fold_in(splits[5], 71), 0),
        "off_blocks": centred(splits[1], (PAIRS, NB, NB), (PANELS * NB) ** -0.5, 0.046875, ((1, 32), (2, 16))),
        "low_factor": noise_with(splits[2], (TRAIL, PANELS, NB), (PANELS * NB) ** -0.5, 0.09375, ((0, 32), (2, 16)), (2, 0, 32, 2.75)),
        "rhs_top": centred(splits[3], (PANELS, NB, R), 1.0, 6.0, ((1, 32),), jnp.float32),
        "rhs_low": centred(splits[4], (TRAIL, R), 1.0, 6.0, ((0, 512),), jnp.float32),
    }


def pair_slot(target, source):
    return target * (target - 1) // 2 + source


def reference(diag_inverse, off_blocks, low_factor, rhs_top, rhs_low):
    solutions = []
    rounded = []
    for panel in range(PANELS):
        current = rhs_top[panel]
        for source in range(panel):
            current = current - jnp.dot(off_blocks[pair_slot(panel, source)], rounded[source], preferred_element_type=jnp.float32)
        solution = jnp.dot(diag_inverse[panel].T, current, precision=lax.Precision.HIGHEST)
        solutions.append(solution)
        rounded.append(solution.astype(jnp.bfloat16))
    stacked = jnp.stack(rounded).reshape(PANELS * NB, R)
    blocks = low_factor.reshape(TRAIL // LOW_DEV, LOW_DEV, PANELS * NB)

    def one_block(factor_rows):
        return jnp.dot(factor_rows, stacked, preferred_element_type=jnp.float32)

    updates = lax.map(one_block, blocks).reshape(TRAIL, R)
    return jnp.stack(solutions), rhs_low - updates
```

```python
import functools

import jax
import jax.numpy as jnp
from jax import lax
from jax.experimental import pallas as pl
from jax.experimental.pallas import tpu as pltpu
from jax.sharding import PartitionSpec as P

MESH = pl.DeviceIdType.MESH
F32 = jnp.float32
BF16 = jnp.bfloat16
PANELS = 8
NZ = 16
NP = 32
COLS = 128
ROWS = 64
SIDES = 256
LOW = 1536
OWN = LOW // NZ
SUB = 2
PIECE = OWN // SUB
DOWN = NZ // 2
UP = NZ - 1 - DOWN


def plane_offsets():
    offsets = [(dy, dx, dc) for dy in range(4) for dx in range(4) for dc in range(2)]
    offsets.remove((0, 0, 0))
    ring = (0, 1, 2, 1)
    return sorted(offsets, key=lambda o: -(ring[o[0]] + ring[o[1]] + 0.5 * o[2]))


def ring_offsets():
    return sorted(range(1, NZ), key=lambda d: -min(d, NZ - d))


def await_bytes(view, sem):
    pltpu.make_async_copy(view, view, sem).wait()


def tiles_of(value):
    rows = value.shape[0]
    left = value[:, :128].reshape(rows // 8, 8, 128)
    right = value[:, 128:].reshape(rows // 8, 8, 128)
    return left, right


def whole_of(tiles):
    count = tiles.shape[0] // 2
    left = tiles[:count].reshape(count * 8, 128)
    right = tiles[count:].reshape(count * 8, 128)
    return jnp.concatenate([left, right], axis=1)


def kernel(
    d_ref, o_ref, low_ref, top_ref, rhs_ref, solved_ref, out_ref,
    stacked, pending, share, share_in, x_tiles, x_low, sums, sums_in, cur_tiles,
    low_in, low_flat, loose, down_out, down_in, up_out, up_in,
    low_sem, share_sem, x_sem, sums_sem, cur_sem, down_sem, up_sem,
    share_send, x_send, sums_send, cur_send, down_send, up_send,
):
    i = lax.axis_index("prow")
    j = lax.axis_index("pcol")
    y, x, core = j // 8, (j // 2) % 4, j % 2

    def plane_peer(offset):
        dy, dx, dc = offset
        return ((y + dy) % 4) * 8 + ((x + dx) % 4) * 2 + (core + dc) % 2

    load_low = pltpu.make_async_copy(low_ref, low_in, low_sem)
    load_low.start()

    barrier = pltpu.get_barrier_semaphore()
    for offset in plane_offsets():
        pl.semaphore_signal(
            barrier, inc=1, device_id=(i, plane_peer(offset)), device_id_type=MESH
        )
    for d in ring_offsets():
        pl.semaphore_signal(
            barrier, inc=1, device_id=((i + d) % NZ, j), device_id_type=MESH
        )

    for k in range(PANELS):
        d = d_ref[k]
        hi = d.astype(BF16).astype(F32)
        lo = d - hi
        terms = jnp.concatenate([hi, hi, lo, lo], axis=0)
        stacked[k] = terms.T.astype(BF16)
    pending[...] = jnp.zeros_like(pending)
    pl.semaphore_wait(barrier, NP - 1 + NZ - 1)

    def diagonal(k, current):
        hi = current.astype(BF16)
        lo = (current - hi.astype(F32)).astype(BF16)
        terms = jnp.concatenate([hi, lo, hi, lo], axis=0)
        product = jnp.dot(stacked[k], terms, preferred_element_type=F32)
        left, right = tiles_of(product)
        share[k, : NP // 2] = left
        share[k, NP // 2 :] = right
        for offset in plane_offsets():
            peer = plane_peer(offset)
            pltpu.make_async_remote_copy(
                src_ref=share.at[k, peer], dst_ref=share_in.at[k, j],
                send_sem=share_send, recv_sem=share_sem.at[k],
                device_id=(i, peer), device_id_type=MESH,
            ).start()
        share_in[k, j] = share[k, j]

    def solve(k):
        await_bytes(share_in.at[k, pl.ds(0, NP - 1)], share_sem.at[k])
        x_tiles[k, j] = jnp.sum(share_in[k], axis=0)
        for offset in plane_offsets():
            peer = plane_peer(offset)
            pltpu.make_async_remote_copy(
                src_ref=x_tiles.at[k, j], dst_ref=x_tiles.at[k, j],
                send_sem=x_send, recv_sem=x_sem.at[k],
                device_id=(i, peer), device_id_type=MESH,
            ).start()

    def gathered(k):
        await_bytes(x_tiles.at[k, pl.ds(0, NP - 1)], x_sem.at[k])
        packed = whole_of(x_tiles[k]).astype(BF16)
        x_low[pl.ds(pl.multiple_of(k * COLS, COLS), COLS), :] = packed
        return packed

    def solved_rows(k):
        half = j // 2
        for c in range(2):
            tile = x_tiles[k, c * (NP // 2) + half]
            solved_ref[k, :, c * 128 : (c + 1) * 128] = jnp.where(
                j % 2 == 0, tile[:4], tile[4:]
            )

    def flatten(b):
        rows = pl.ds(pl.multiple_of(b * OWN, OWN), OWN)
        loose[...] = low_in[rows].astype(F32).reshape(OWN * PANELS, COLS)
        for k in range(PANELS):
            low_flat[rows, k * COLS : (k + 1) * COLS] = loose[
                pl.ds(k, OWN, stride=PANELS), :
            ].astype(BF16)

    diagonal(0, top_ref[0])
    load_low.wait()

    def panel_step(k, carry):
        flatten(2 * k)
        solve(k)
        flatten(2 * k + 1)
        packed = gathered(k)
        t = k + 1
        slot = t * (t - 1) // 2 + k
        update = pending[t] + jnp.dot(o_ref[slot], packed, preferred_element_type=F32)
        left, right = tiles_of(update)
        sums[t, : NZ // 2] = left
        sums[t, NZ // 2 :] = right
        for d in ring_offsets():
            peer = (i + d) % NZ
            pltpu.make_async_remote_copy(
                src_ref=sums.at[t, peer], dst_ref=sums_in.at[t, i],
                send_sem=sums_send, recv_sem=sums_sem.at[t],
                device_id=(peer, j), device_id_type=MESH,
            ).start()
        sums_in[t, i] = sums[t, i]

        def later(u, c):
            other = u * (u - 1) // 2 + k
            pending[u] = pending[u] + jnp.dot(
                o_ref[other], packed, preferred_element_type=F32
            )
            return c

        lax.fori_loop(k + 2, PANELS, later, 0)
        solved_rows(k)

        await_bytes(sums_in.at[t, pl.ds(0, NZ - 1)], sums_sem.at[t])
        row = pl.multiple_of((i % 8) * 8, 8)
        rhs = jnp.where(
            i < 8, top_ref[t, pl.ds(row, 8), :128], top_ref[t, pl.ds(row, 8), 128:]
        )
        cur_tiles[t, i] = rhs - jnp.sum(sums_in[t], axis=0)
        for d in ring_offsets():
            peer = (i + d) % NZ
            pltpu.make_async_remote_copy(
                src_ref=cur_tiles.at[t, i], dst_ref=cur_tiles.at[t, i],
                send_sem=cur_send, recv_sem=cur_sem.at[t],
                device_id=(peer, j), device_id_type=MESH,
            ).start()
        await_bytes(cur_tiles.at[t, pl.ds(0, NZ - 1)], cur_sem.at[t])
        diagonal(t, whole_of(cur_tiles[t]))
        return carry

    lax.fori_loop(0, PANELS - 1, panel_step, 0)
    last = PANELS - 1
    flatten(2 * last)
    solve(last)
    flatten(2 * last + 1)
    gathered(last)

    def term(owner):
        rows = pl.ds(pl.multiple_of(owner * OWN, OWN), OWN)
        return jnp.dot(low_flat[rows, :], x_low[...], preferred_element_type=F32)

    below, above = (i + NZ - 1) % NZ, (i + 1) % NZ

    def hop(step, owner, outgoing, incoming, send, recv, peer):
        own = term(owner)
        for q in range(SUB):
            part = pl.ds(q * PIECE, PIECE)
            value = own[q * PIECE : (q + 1) * PIECE]
            if step:
                await_bytes(incoming.at[step - 1, part], recv.at[step - 1, q])
                value = value + incoming[step - 1, part, :]
            outgoing[step, part, :] = value
            pltpu.make_async_remote_copy(
                src_ref=outgoing.at[step, part], dst_ref=incoming.at[step, part],
                send_sem=send, recv_sem=recv.at[step, q],
                device_id=(peer, j), device_id_type=MESH,
            ).start()

    for step in range(DOWN):
        hop(step, (i + DOWN + step) % NZ, down_out, down_in, down_send, down_sem, below)
        if step < UP:
            hop(step, (i + UP - step) % NZ, up_out, up_in, up_send, up_sem, above)
    solved_rows(last)
    own = term(i)
    for q in range(SUB):
        part = pl.ds(q * PIECE, PIECE)
        await_bytes(up_in.at[UP - 1, part], up_sem.at[UP - 1, q])
        await_bytes(down_in.at[DOWN - 1, part], down_sem.at[DOWN - 1, q])
        out_ref[part, :] = rhs_ref[part, :] - (
            own[q * PIECE : (q + 1) * PIECE]
            + up_in[UP - 1, part, :]
            + down_in[DOWN - 1, part, :]
        )

    await_bytes(share_in.at[:, pl.ds(0, NP - 1)], share_send)
    await_bytes(x_tiles.at[:, pl.ds(0, NP - 1)], x_send)
    await_bytes(sums_in.at[pl.ds(1, PANELS - 1), pl.ds(0, NZ - 1)], sums_send)
    await_bytes(cur_tiles.at[pl.ds(1, PANELS - 1), pl.ds(0, NZ - 1)], cur_send)
    await_bytes(down_in, down_send)
    await_bytes(up_in, up_send)


def on_device(diag_inverse, off_blocks, low_factor, rhs_top, rhs_low):
    vmem = pl.BlockSpec(memory_space=pltpu.VMEM)
    dma = pltpu.SemaphoreType.DMA
    return pl.pallas_call(
        kernel,
        out_shape=(
            jax.ShapeDtypeStruct((PANELS, ROWS // NZ, SIDES), F32),
            jax.ShapeDtypeStruct((OWN, SIDES), F32),
        ),
        in_specs=[vmem, vmem, pl.BlockSpec(memory_space=pl.ANY), vmem, vmem],
        out_specs=(vmem, vmem),
        scratch_shapes=[
            pltpu.VMEM((PANELS, COLS, 4 * ROWS), BF16),
            pltpu.VMEM((PANELS, ROWS, SIDES), F32),
            pltpu.VMEM((PANELS, NP, 8, 128), F32),
            pltpu.VMEM((PANELS, NP, 8, 128), F32),
            pltpu.VMEM((PANELS, NP, 8, 128), F32),
            pltpu.VMEM((PANELS * COLS, SIDES), BF16),
            pltpu.VMEM((PANELS, NZ, 8, 128), F32),
            pltpu.VMEM((PANELS, NZ, 8, 128), F32),
            pltpu.VMEM((PANELS, NZ, 8, 128), F32),
            pltpu.VMEM((LOW, PANELS, COLS), BF16),
            pltpu.VMEM((LOW, PANELS * COLS), BF16),
            pltpu.VMEM((OWN * PANELS, COLS), F32),
            pltpu.VMEM((DOWN, OWN, SIDES), F32),
            pltpu.VMEM((DOWN, OWN, SIDES), F32),
            pltpu.VMEM((UP, OWN, SIDES), F32),
            pltpu.VMEM((UP, OWN, SIDES), F32),
            dma,
            dma((PANELS,)), dma((PANELS,)), dma((PANELS,)), dma((PANELS,)),
            dma((DOWN, SUB)), dma((UP, SUB)),
            dma, dma, dma, dma, dma, dma,
        ],
        compiler_params=pltpu.CompilerParams(
            collective_id=0, has_side_effects=True, vmem_limit_bytes=48 * 2**20
        ),
    )(diag_inverse, off_blocks, low_factor, rhs_top, rhs_low)


def solution(mesh):
    placed = (
        P(None, "pcol", "prow"),
        P(None, "pcol", "prow"),
        P("pcol", None, "prow"),
        P(None, "pcol", None),
        P(("pcol", "prow"), None),
    )
    return jax.shard_map(
        on_device,
        mesh=mesh,
        in_specs=placed,
        out_specs=(P(None, ("prow", "pcol"), None), P(("pcol", "prow"), None)),
        check_vma=False,
    )
```
